32 devices in a mesh: row: 2 (over core), col: 4 (over y, x), layer: 4 (over z).
Axes of the slice: x: 2, y: 2, z: 4, core: 2. Of those that a mesh axis runs over, the one named last changes fastest.
Arguments:
- left_mant: bfloat16 [3, 5, 6, 1024, 4, 256], P(None, None, None, ('row', 'col'), 'layer'), may hold values from 9.983778e-07 to 1
- right_mant: bfloat16 [3, 5, 6, 4, 256, 1024], P(None, None, None, 'layer', 'row', 'col'), may hold values from 9.983778e-07 to 1
- left_scale: float32 [3, 5], replicated, may hold values from -750 to 0
- right_scale: float32 [3, 5], replicated, may hold values from -750 to 0
- rule_probs: float32 [6, 6, 6], replicated, may hold values from 0.05 to 1
- pair_logp: float32 [6, 4, 4], replicated, may hold values from -4 to 4
- nucleotides: int32 [65536], replicated, may hold values from 0 to 3
- first_block: int32 [1], replicated, may hold values from 0 to 55
Outputs:
- block_values: float32 [3, 6, 1024, 1024], P(None, None, ('row', 'layer'), 'col')
- block_scale: float32 [3], replicated
The draws below stay inside these ranges and needn't reach their ends.
All inputs are finite; a program needn't handle non-finite values.
Results may differ from the reference program's by a relative error of at most 0.0003.
Values may be sent and summed in bfloat16 or wider, within the bound.
A program may use at most 128 MiB of HBM per device.

```python
import math
import jax
import jax.numpy as jnp
from jax import lax

NT = 6
BLK = 1024
SPLITS = 5
NOUT = 3
LENGTH = 65536
KGROUPS = 4
KWIDTH = 256


def scale_levels(key):
    stepping = jax.random.uniform(jax.random.fold_in(key, 11), (NOUT + SPLITS + 1,), jnp.float32, -150.0, -60.0)
    return jnp.concatenate([jnp.zeros((1,), jnp.float32), jnp.cumsum(stepping)])


def scale_jitter(key, salt):
    return jax.random.uniform(jax.random.fold_in(key, salt), (NOUT, SPLITS), jnp.float32, 0.0, 1.5)


def draw_left_scale(key, part):
    levels = scale_levels(key)
    starts = jnp.arange(NOUT)[:, None]
    reaches = jnp.arange(1, SPLITS + 1)[None, :]
    return levels[starts + reaches] - levels[starts] + scale_jitter(key, 23)


def draw_right_scale(key, part):
    levels = scale_levels(key)
    starts = jnp.arange(NOUT)[:, None]
    reaches = jnp.arange(1, SPLITS + 1)[None, :]
    return levels[starts + SPLITS + 1] - levels[starts + reaches] + scale_jitter(key, 37)


def with_ends(drawn, stream_key, low, largest):
    spot = [jax.random.randint(jax.random.fold_in(stream_key, axis), (), 0, length) for axis, length in enumerate(drawn.shape)]
    main_axis = drawn.shape.index(max(drawn.shape))
    beside = spot[:main_axis] + [(spot[main_axis] + 1) % drawn.shape[main_axis]] + spot[main_axis + 1:]
    return drawn.at[tuple(spot)].set(low).at[tuple(beside)].set(largest)


def block_levels(key, extent, cuts, smallest, top_value):
    factor_of, own = 1.0, jax.random.fold_in(key, 6)
    for dim, shards_of in cuts:
        draws = jnp.exp(jax.random.uniform(jax.random.fold_in(own, dim), (shards_of,), jnp.float32, smallest / len(cuts), top_value / len(cuts)))
        factor_of = factor_of * jnp.repeat(draws, extent[dim] // shards_of).reshape([-1 if axis == dim else 1 for axis in range(len(extent))])
    return factor_of


def centred(key, dims, width, limit, dtype=jnp.bfloat16):
    drawn = jax.random.normal(key, dims, jnp.float32) * width
    return jnp.minimum(jnp.maximum(drawn, -limit), limit).astype(dtype)


def setup_inputs(seed: int = 0) -> dict:
    key_of = jax.random.split(jax.random.key(seed), 9)
    return {
        "left_mant": jnp.clip(jnp.exp(math.log(1.0) - 13.817134 * jax.random.uniform(key_of[0], (NOUT, SPLITS, NT, BLK, KGROUPS, KWIDTH), jnp.float32) ** block_levels(key_of[0], (NOUT, SPLITS, NT, BLK, KGROUPS, KWIDTH), ((3, 8), (4, 4)), -0.2, 0.2)), 9.98377799987793e-07, 1.0).astype(jnp.bfloat16),
        "right_mant": jnp.clip(jnp.exp(math.log(1.0) - 13.817134 * jax.random.uniform(key_of[1], (NOUT, SPLITS, NT, KGROUPS, KWIDTH, BLK), jnp.float32) ** block_levels(key_of[1], (NOUT, SPLITS, NT, KGROUPS, KWIDTH, BLK), ((3, 4), (4, 2), (5, 4)), -0.2, 0.2)), 9.98377799987793e-07, 1.0).astype(jnp.bfloat16),
        "left_scale": draw_left_scale(jax.random.fold_in(key_of[8], 71), 0),
        "right_scale": draw_right_scale(jax.random.fold_in(key_of[8], 71), 0),
        "rule_probs": jnp.clip(jnp.exp(jax.random.uniform(key_of[4], (NT, NT, NT), jnp.float32, math.log(0.05), math.log(1.0))), 0.05, 1.0),
        "pair_logp": centred(key_of[5], (NT, 4, 4), 1.0, 4.0, jnp.float32),
        "nucleotides": with_ends(jax.random.randint(key_of[6], (LENGTH,), 0, 4), jax.random.fold_in(key_of[6], 1), 0, 3).astype(jnp.int32),
        "first_block": jax.random.randint(key_of[7], (1,), 0, LENGTH // BLK - NOUT - SPLITS).astype(jnp.int32),
    }


def reference(left_mant, right_mant, left_scale, right_scale, rule_probs, pair_logp, nucleotides, first_block):
    total_scale = left_scale + right_scale
    highest = jnp.max(total_scale, axis=1)
    weight = jnp.exp(total_scale - highest[:, None])
    mixing = (rule_probs[None, None] * weight[:, :, None, None, None]).astype(jnp.bfloat16)
    inside_list = []
    for block_id in range(NOUT):
        summed = jnp.zeros((NT, BLK, BLK), jnp.float32)
        for split_id in range(SPLITS):
            left_block = left_mant[block_id, split_id].reshape(NT, BLK, BLK)
            right_block = right_mant[block_id, split_id].reshape(NT, BLK, BLK)
            mixed_part = jnp.einsum("xyz,yik->xzik", mixing[block_id, split_id].astype(jnp.float32), left_block.astype(jnp.float32), precision=lax.Precision.HIGHEST).astype(jnp.bfloat16)
            summed = summed + jnp.einsum("xzik,zkj->xij", mixed_part.astype(jnp.float32), right_block.astype(jnp.float32), precision=lax.Precision.HIGHEST)
        row_start = ((first_block[0] + block_id) * BLK).astype(jnp.int32)
        col_start = ((first_block[0] + block_id + SPLITS + 1) * BLK).astype(jnp.int32)
        row_codes = lax.dynamic_slice_in_dim(nucleotides, row_start, BLK)
        col_codes = lax.dynamic_slice_in_dim(nucleotides, col_start, BLK)
        pairing = pair_logp[:, row_codes[:, None], col_codes[None, :]]
        inside_list.append(highest[block_id] + jnp.log(summed) + pairing)
    inside = jnp.stack(inside_list)
    peak_value = jnp.max(inside, axis=(1, 2, 3))
    return inside - peak_value[:, None, None, None], peak_value
```

```python
from functools import partial

import jax
import jax.numpy as jnp
from jax import lax
from jax.experimental import pallas as pl
from jax.experimental.pallas import tpu as pltpu
from jax.sharding import PartitionSpec as P


TILE = 32
VMEM_BYTES = 63 * 1024 * 1024


def add_pieces(left_full, mix_block, running, arrived, anchor):
    channels = arrived.shape[1]

    def one_split(split_id, partial_sum):
        left_part = lax.dynamic_index_in_dim(left_full, split_id, 0, False)
        mixing_now = lax.dynamic_index_in_dim(mix_block, split_id, 0, False)
        mixed_part = jnp.einsum(
            "xyz,yiqn->xziqn", mixing_now, left_part, preferred_element_type=jnp.float32
        ).astype(jnp.bfloat16)
        mixed_part = mixed_part.reshape(channels, channels, left_part.shape[1], -1)
        right_part = lax.dynamic_index_in_dim(arrived, split_id, 0, False)
        right_part = right_part.reshape(channels, -1, right_part.shape[3])
        return partial_sum + jnp.einsum(
            "xzik,zkj->xij", mixed_part, right_part, preferred_element_type=jnp.float32
        )

    return lax.fori_loop(0, arrived.shape[0], one_split, running)


def take_codes(nucleotides, length, position):
    return lax.dynamic_slice_in_dim(nucleotides, position, length)


def local(
    left_mant, right_mant, left_scale, right_scale, rule_probs, pair_logp, nucleotides, first_block
):
    total_scale = left_scale + right_scale
    highest = jnp.max(total_scale, axis=1)
    weight = jnp.exp(total_scale - highest[:, None])
    mixing = (rule_probs[None, None] * weight[:, :, None, None, None]).astype(jnp.bfloat16)
    count_out = left_mant.shape[0]
    count_split = left_mant.shape[1]
    channels = left_mant.shape[2]
    layers = lax.axis_size("layer")
    partials = []
    for block_id in range(count_out):
        left_rows_all = lax.all_gather(left_mant[block_id], "col", axis=2, tiled=True)
        right_ready = right_mant[block_id]
        accumulate = partial(add_pieces, left_rows_all, mixing[block_id])
        zeroed = jnp.zeros((channels, left_rows_all.shape[2], right_ready.shape[4]), jnp.float32)
        partials.append(
            accumulate(zeroed, lax.all_gather(right_ready, "row", axis=3, tiled=True), jnp.int32(0))
        )
    summed = jnp.stack(partials)
    summed = lax.psum_scatter(summed, "layer", scatter_dimension=2, tiled=True)
    rows_final = summed.shape[2]
    cols_final = summed.shape[3]
    block_len = cols_final * lax.axis_size("col")
    row_anchor = (lax.axis_index("row") * layers + lax.axis_index("layer")) * rows_final
    col_anchor = lax.axis_index("col") * cols_final
    offsets = jnp.arange(count_out, dtype=jnp.int32) + first_block[0]
    row_codes = jax.vmap(partial(take_codes, nucleotides, rows_final))(
        offsets * block_len + row_anchor
    )
    col_codes = jax.vmap(partial(take_codes, nucleotides, cols_final))(
        (offsets + count_split + 1) * block_len + col_anchor
    )
    symbols = jnp.arange(4, dtype=jnp.int32)
    row_hot = (row_codes[:, :, None] == symbols).astype(jnp.float32)
    col_hot = (col_codes[:, :, None] == symbols).astype(jnp.float32)
    pairing = jnp.einsum(
        "biu,xuv,bjv->bxij", row_hot, pair_logp, col_hot, precision=lax.Precision.HIGHEST
    )
    inside = highest[:, None, None, None] + jnp.log(summed) + pairing
    peak_value = lax.pmax(jnp.max(inside, axis=(1, 2, 3)), ("row", "col", "layer"))
    return (inside - peak_value[:, None, None, None], peak_value)


MESH = pl.DeviceIdType.MESH
LAG = 2


def flip(first, second):
    low = lax.rem(first + second, 2)
    high = lax.rem(first // 2 + second // 2, 2)
    return low + 2 * high


def fused(
    sizes, left_ref, right_ref, spread_ref, chosen_ref, codes_ref, out_ref, peak_ref,
    lefts, rights, sums, landed, landed_top, mixed, expand, peaks,
    own_sem, right_sem, right_send, right_recv, side_send, side_recv, pass_send, pass_recv,
    sum_send, sum_recv, top_recv, peak_send, peak_recv, out_sem,
):
    count_out, count_split, channels, rows, width, depth, cols, tile = sizes
    row, col, layer = lax.axis_index("row"), lax.axis_index("col"), lax.axis_index("layer")
    other = 1 - row
    sides = (flip(col, 1), flip(col, 2))
    half = channels // 2
    total = count_out * 4

    barrier = pltpu.get_barrier_semaphore()
    greeted = [{"row": other}, {"col": sides[0]}, {"col": sides[1]}]
    greeted += [{"layer": lax.rem(layer + step, 4)} for step in (1, 2, 3)]
    for device in greeted:
        pl.semaphore_signal(barrier, inc=1, device_id=device, device_id_type=MESH)
    pl.semaphore_wait(barrier, len(greeted))

    def own_copy(b):
        return pltpu.make_async_copy(left_ref.at[b], lefts.at[b, 0], own_sem.at[b])

    def right_copy(b):
        place = rights.at[b, :, :, pl.ds(pl.multiple_of(row * depth, depth), depth)]
        return pltpu.make_async_copy(right_ref.at[b], place, right_sem.at[b])

    def right_share(b):
        place = rights.at[b, :, :, pl.ds(pl.multiple_of(row * depth, depth), depth)]
        return pltpu.make_async_remote_copy(
            right_ref.at[b], place, right_send.at[b], right_recv.at[b],
            device_id={"row": other}, device_id_type=MESH,
        )

    def side_share(b, side, part):
        return pltpu.make_async_remote_copy(
            left_ref.at[b, :, pl.ds(part * half, half)],
            lefts.at[b, side + 1, :, pl.ds(part * half, half)],
            side_send.at[b, side, part], side_recv.at[b, side, part],
            device_id={"col": sides[side]}, device_id_type=MESH,
        )

    def pass_on(b, side):
        return pltpu.make_async_remote_copy(
            lefts.at[b, side + 1, :, pl.ds(side * half, half)],
            lefts.at[b, 3, :, pl.ds(side * half, half)],
            pass_send.at[b, side], pass_recv.at[b, side],
            device_id={"col": sides[1 - side]}, device_id_type=MESH,
        )

    def start_block(b):
        right_share(b).start()
        for part in (0, 1):
            for side in (0, 1):
                side_share(b, side, part if side == 0 else 1 - part).start()
        own_copy(b).start()
        right_copy(b).start()

    def sum_share(b, slot, up):
        return pltpu.make_async_remote_copy(
            sums.at[b, slot], landed.at[b, slot], sum_send.at[b, slot], sum_recv.at[b, slot],
            device_id={"layer": lax.rem(layer + (1 if up else 3), 4)}, device_id_type=MESH,
        )

    def sum_share_top(b, slot):
        return pltpu.make_async_remote_copy(
            sums.at[b, slot], landed_top.at[b], sum_send.at[b, slot], top_recv.at[b],
            device_id={"layer": lax.rem(layer + 3, 4)}, device_id_type=MESH,
        )

    def add_landed(b, slot, source):
        def add(x, carry):
            sums[b, slot, x] = sums[b, slot, x] + source[x]
            return carry
        lax.fori_loop(0, channels, add, 0)

    def relay(index, hop):
        b, slot = index // 4, lax.rem(index, 4)
        owner = flip(col, slot)

        def arrive():
            if hop:
                sum_share(b, slot, True).wait_recv()
                add_landed(b, slot, landed.at[b, slot])

        @pl.when((owner > layer) & (layer == hop))
        def _():
            arrive()
            sum_share(b, slot, True).start()

        @pl.when((owner < layer) & (3 - layer == hop))
        def _():
            arrive()

            @pl.when(owner == layer - 1)
            def _():
                sum_share_top(b, slot).start()

            @pl.when(owner < layer - 1)
            def _():
                sum_share(b, slot, False).start()

    same = (
        lax.broadcasted_iota(jnp.int32, (tile, channels * tile), 0)
        == lax.rem(lax.broadcasted_iota(jnp.int32, (tile, channels * tile), 1), tile)
    )

    def compute(b, slot):
        def one_split(s, carry):
            for zx in range(channels * channels):
                line = spread_ref[b * count_split + s, zx:zx + 1, :]
                expand[zx * tile:(zx + 1) * tile, :] = jnp.where(same, line, 0.0).astype(jnp.bfloat16)

            def one_tile(i, carry):
                start = pl.multiple_of(i * tile, tile)
                piece = lefts[b, slot, s, :, pl.ds(start, tile), :].reshape(channels * tile, width)
                whole = jnp.dot(expand[...], piece, preferred_element_type=jnp.float32)
                whole = whole.astype(jnp.bfloat16)
                for z in range(channels):
                    for x in range(channels):
                        at = (z * channels + x) * tile
                        mixed[pl.ds(x * rows + start, tile), z * width:(z + 1) * width] = whole[at:at + tile]
                return carry

            lax.fori_loop(0, rows // tile, one_tile, 0)
            right = rights[b, s].reshape(channels * width, cols)
            for x in range(channels):
                term = jnp.dot(
                    mixed[x * rows:(x + 1) * rows, :], right, preferred_element_type=jnp.float32
                )
                before = jnp.where(s == 0, 0.0, sums[b, slot, x])
                sums[b, slot, x] = before + term
            return carry

        lax.fori_loop(0, count_split, one_split, 0)

    peaks[0] = jnp.full_like(peaks[0], -jnp.inf)

    def finish(b):
        slot = flip(col, layer)

        @pl.when(layer > 0)
        def _():
            sum_share(b, slot, True).wait_recv()
            add_landed(b, slot, landed.at[b, slot])

        @pl.when(layer < 3)
        def _():
            sum_share_top(b, slot).wait_recv()
            add_landed(b, slot, landed_top.at[b])

        def one_channel(x, best):
            code = codes_ref[b]
            pairing = chosen_ref[b, x, 3:4, :]
            for u in (2, 1, 0):
                pairing = jnp.where(code == u, chosen_ref[b, x, u:u + 1, :], pairing)
            value = jnp.log(sums[b, slot, x]) + pairing
            sums[b, slot, x] = value
            return jnp.maximum(best, jnp.max(value, axis=0, keepdims=True))

        best = lax.fori_loop(0, channels, one_channel, jnp.full((1, cols), -jnp.inf, jnp.float32))
        best = jnp.max(best, axis=1, keepdims=True)
        at = lax.broadcasted_iota(jnp.int32, peaks.shape[1:], 0)
        peaks[0] = jnp.where(at == b, best, peaks[0])

    start_block(0)

    def step(t, carry):
        b, slot = t // 4, lax.rem(t, 4)

        @pl.when((slot == 0) & (t >= 8))
        def _():
            finish(b - 2)

        @pl.when(t < total)
        def _():
            @pl.when(slot == 0)
            def _():
                own_copy(b).wait()
                right_copy(b).wait()
                right_share(b).wait_recv()

            @pl.when(slot == 1)
            def _():
                side_share(b, 0, 0).wait_recv()
                pass_on(b, 0).start()
                side_share(b, 1, 1).wait_recv()
                pass_on(b, 1).start()

                @pl.when(b < count_out - 1)
                def _():
                    start_block(b + 1)

                side_share(b, 0, 1).wait_recv()

            @pl.when(slot == 2)
            def _():
                side_share(b, 1, 0).wait_recv()

            @pl.when(slot == 3)
            def _():
                pass_on(b, 0).wait_recv()
                pass_on(b, 1).wait_recv()

            compute(b, slot)
            relay(t, 0)

        for hop in (1, 2):
            @pl.when((t >= hop * LAG) & (t - hop * LAG < total))
            def _(hop=hop):
                relay(t - hop * LAG, hop)
        return carry

    lax.fori_loop(0, total + 4, step, 0)
    finish(count_out - 1)

    def swap(number, device):
        copy = pltpu.make_async_remote_copy(
            peaks.at[number], peaks.at[4 + number], peak_send.at[number], peak_recv.at[number],
            device_id=device, device_id_type=MESH,
        )
        copy.start()
        copy.wait()
        peaks[number + 1] = jnp.maximum(peaks[number], peaks[4 + number])

    swap(0, {"row": other})
    swap(1, {"col": sides[0]})
    swap(2, {"col": sides[1]})
    copies = []
    for distance in (1, 2, 3):
        copy = pltpu.make_async_remote_copy(
            peaks.at[3], peaks.at[6 + distance], peak_send.at[2 + distance], peak_recv.at[2 + distance],
            device_id={"layer": lax.rem(layer + distance, 4)}, device_id_type=MESH,
        )
        copy.start()
        copies.append(copy)
    top = peaks[3]
    for distance, copy in zip((1, 2, 3), copies):
        copy.wait()
        top = jnp.maximum(top, peaks[6 + distance])
    peak_ref[...] = top

    slot = flip(col, layer)
    outs = []
    for b in range(count_out):
        level = top[b:b + 1, 0:1]

        def lower(x, carry):
            sums[b, slot, x] = sums[b, slot, x] - level
            return carry

        lax.fori_loop(0, channels, lower, 0)
        copy = pltpu.make_async_copy(sums.at[b, slot], out_ref.at[b], out_sem.at[b])
        copy.start()
        outs.append(copy)

    def settle(b, carry):
        right_share(b).wait_send()
        for side in (0, 1):
            pass_on(b, side).wait_send()
            for part in (0, 1):
                side_share(b, side, part).wait_send()
        for slot in range(4):
            @pl.when(flip(col, slot) != layer)
            def _(slot=slot):
                sum_share(b, slot, True).wait_send()
        return carry

    lax.fori_loop(0, count_out, settle, 0)
    for copy in outs:
        copy.wait()


def local_fused(
    left_mant, right_mant, left_scale, right_scale, rule_probs, pair_logp, nucleotides, first_block
):
    total_scale = left_scale + right_scale
    highest = jnp.max(total_scale, axis=1)
    weight = jnp.exp(total_scale - highest[:, None])
    mixing = (rule_probs[None, None] * weight[:, :, None, None, None]).astype(jnp.bfloat16)
    count_out, count_split, channels, rows, _, width = left_mant.shape
    depth, cols = right_mant.shape[4:]
    tile = TILE
    row, col, layer = lax.axis_index("row"), lax.axis_index("col"), lax.axis_index("layer")
    block_len = cols * lax.axis_size("col")

    spread = mixing.astype(jnp.float32).transpose(0, 1, 4, 2, 3)
    spread = spread.reshape(count_out * count_split, channels * channels, channels, 1)
    spread = jnp.broadcast_to(spread, spread.shape[:3] + (tile,))
    spread = spread.reshape(count_out * count_split, channels * channels, channels * tile)

    by_block = nucleotides.reshape(-1, block_len)
    row_anchor = (row * lax.axis_size("layer") + layer) * rows
    row_codes = lax.dynamic_slice(by_block, (first_block[0], row_anchor), (count_out, rows))
    col_codes = lax.dynamic_slice(
        by_block, (first_block[0] + count_split + 1, col * cols), (count_out, cols)
    )
    codes = jnp.broadcast_to(row_codes[:, :, None], (count_out, rows, cols))
    seen = col_codes[:, None, None, :]
    pairs = pair_logp[None, :, :, :, None]
    chosen = pairs[:, :, :, 3]
    for v in (2, 1, 0):
        chosen = jnp.where(seen == v, pairs[:, :, :, v], chosen)

    sizes = (count_out, count_split, channels, rows, width, depth, cols, tile)
    f32, bf16 = jnp.float32, jnp.bfloat16
    in_vmem = pl.BlockSpec(memory_space=pltpu.VMEM)
    anywhere = pl.BlockSpec(memory_space=pl.ANY)
    dma = pltpu.SemaphoreType.DMA
    flops = 2 * count_out * count_split * channels * channels * 4 * rows * width * cols
    values, peaks = pl.pallas_call(
        partial(fused, sizes),
        out_shape=(
            jax.ShapeDtypeStruct((count_out, channels, rows, cols), f32),
            jax.ShapeDtypeStruct((8, 128), f32),
        ),
        in_specs=[anywhere, anywhere, in_vmem, in_vmem, in_vmem],
        out_specs=(anywhere, in_vmem),
        scratch_shapes=[
            pltpu.VMEM((count_out, 4, count_split, channels, rows, width), bf16),
            pltpu.VMEM((count_out, count_split, channels, width, cols), bf16),
            pltpu.VMEM((count_out, 4, channels, rows, cols), f32),
            pltpu.VMEM((count_out, 4, channels, rows, cols), f32),
            pltpu.VMEM((count_out, channels, rows, cols), f32),
            pltpu.VMEM((channels * rows, channels * width), bf16),
            pltpu.VMEM((channels * channels * tile, channels * tile), bf16),
            pltpu.VMEM((10, 8, 128), f32),
            dma((count_out,)), dma((count_out,)), dma((count_out,)), dma((count_out,)),
            dma((count_out, 2, 2)), dma((count_out, 2, 2)),
            dma((count_out, 2)), dma((count_out, 2)),
            dma((count_out, 4)), dma((count_out, 4)), dma((count_out,)),
            dma((6,)), dma((6,)), dma((count_out,)),
        ],
        compiler_params=pltpu.CompilerParams(
            collective_id=0, has_side_effects=True, vmem_limit_bytes=VMEM_BYTES
        ),
        cost_estimate=pl.CostEstimate(
            flops=flops, bytes_accessed=left_mant.size * 8, transcendentals=count_out * channels * rows * cols
        ),
    )(
        left_mant.reshape(count_out, count_split, channels, rows, width),
        right_mant.reshape(count_out, count_split, channels, depth, cols),
        spread, chosen, codes,
    )
    return values, peaks[:count_out, 0] + highest


def fits_fused(shape, args):
    left, right = args[0].shape, args[1].shape
    rows, depth, cols = left[3] // (shape["row"] * shape["col"]), right[4] // shape["row"], right[5] // shape["col"]
    return (
        shape["row"] == 2 and shape["col"] == 4 and shape["layer"] == 4
        and left[4] == 4 and right[3] == 4 and left[0] <= 3 and left[2] % 2 == 0
        and rows * 8 == left[3] and rows % TILE == 0 and depth % 16 == 0 and left[5] == 2 * depth
        and left[5] % 128 == 0 and cols % 128 == 0 and left[3] == right[5]
        and left[0] * left[1] * left[2] * rows * left[5] <= VMEM_BYTES // 20
    )


def solution(mesh):
    in_specs = (
        P(None, None, None, ("row", "col"), "layer", None),
        P(None, None, None, "layer", "row", "col"),
        P(),
        P(),
        P(),
        P(),
        P(),
        P(),
    )
    out_specs = (P(None, None, ("row", "layer"), "col"), P())

    def whole(*args):
        body = local_fused if fits_fused(mesh.shape, args) else local
        return jax.shard_map(
            body, mesh=mesh, in_specs=in_specs, out_specs=out_specs, check_vma=False
        )(*args)

    return whole
```
